512 devices in a mesh: ctx: 64 (over x, z_lo, core), head: 8 (over y, z_hi).
Axes of the slice: x: 4, y: 4, z: 16 (z_hi: 2, z_lo: 8; z = z_hi * 8 + z_lo), core: 2. Of those that a mesh axis runs over, the one named last changes fastest.
Arguments:
- queries: bfloat16 [32768, 2048], P('ctx', 'head'), may hold values from -64 to 64
- keys: bfloat16 [32768, 2048], P('ctx', 'head'), may hold values from -32 to 32
- values: bfloat16 [32768, 2048], P('ctx', 'head'), may hold values from -6 to 6
- dates: int32 [32768], P('ctx'), may hold values from 0 to 15, as said below
- plan: int32 [2], replicated, may hold values from 1 to 63, as said below
- out_weight: bfloat16 [2048, 2048], P('head'), may hold values from -0.1875 to 0.1875
Outputs:
- projected: bfloat16 [32768, 2048], P('ctx', 'head')
The draws below stay inside these ranges and needn't reach their ends.
Inputs may be any that keep to these rules, and one draw needn't show every extreme that they name: `dates`: nondecreasing along the sequence; every date occurs. `plan`: the 2 entries differ; one of them is 63.
All inputs are finite; a program needn't handle non-finite values.
Results may differ from the reference program's by a relative error of at most 0.017.
Values may be sent and summed in bfloat16 or wider, within the bound.
A program may use at most 64 MiB of HBM per device.

```python
import jax
import jax.numpy as jnp
from jax import lax

HEADS = 16
HEAD_DIM = 128
D = 2048
TOK_DEV = 512
TOKENS = 32768
DATES = 16
ROUNDS = 2
N_CTX = 64
N_HEAD = 8


def draw_queries(key, part):
    key = jax.random.fold_in(key, 11)
    drawn = jax.random.normal(key, (TOKENS, D), jnp.float32)
    return drawn.astype(jnp.bfloat16)


def draw_keys(key, part):
    key = jax.random.fold_in(key, 12)
    drawn = jax.random.normal(key, (TOKENS, D), jnp.float32)
    return drawn.astype(jnp.bfloat16)


def draw_dates(key, part):
    key = jax.random.fold_in(key, 3)
    cuts = jax.random.permutation(key, TOKENS - 1)[:DATES - 1] + 1
    positions = jnp.arange(TOKENS, dtype=jnp.int32)
    return jnp.sum((positions[:, None] >= cuts[None, :]).astype(jnp.int32), axis=1).astype(jnp.int32)


def draw_plan(key, part):
    key = jax.random.fold_in(key, 5)
    other = jax.random.randint(key, (), 1, N_CTX - 1, jnp.int32)
    order = jax.random.randint(jax.random.fold_in(key, 1), (), 0, 2, jnp.int32)
    widest = jnp.int32(N_CTX - 1)
    return jnp.where(order == 0, jnp.stack([other, widest]), jnp.stack([widest, other])).astype(jnp.int32)


def spiked(result, own_key, source, target, shards_of, factor):
    owner, partner = [(jnp.arange(result.shape[axis_at]) // (result.shape[axis_at] // shards_of)).reshape([-1 if axis == axis_at else 1 for axis in range(result.ndim)]) for axis_at in (source, target)]
    chosen = jax.random.permutation(own_key, shards_of)[partner]
    strong = (owner == chosen) | (owner == (partner + shards_of // 2) % shards_of)
    return jnp.where(strong, factor * result, result)


def block_scale(rng, extent, pieces, least, top_value):
    level, own = 1.0, jax.random.fold_in(rng, 6)
    for axis_at, blocks in pieces:
        draws = jnp.exp(jax.random.uniform(jax.random.fold_in(own, axis_at), (blocks,), jnp.float32, least / len(pieces), top_value / len(pieces)))
        level = level * jnp.repeat(draws, extent[axis_at] // blocks).reshape([-1 if axis == axis_at else 1 for axis in range(len(extent))])
    return level


def bell_draw(own_key, dims, width, reach, split=(), kind=jnp.bfloat16):
    values = jax.random.normal(own_key, dims, jnp.float32) * width
    if len(split) > 0:
        values = block_scale(own_key, dims, split, -0.22, 0.18) * values
    return jnp.clip(values, min=-reach, max=reach).astype(kind)


def bell_draw_with(own_key, extent, deviation, reach, shards, heavy, kind=jnp.bfloat16):
    values = deviation * jax.random.normal(own_key, extent, jnp.float32)
    if shards:
        values = values * block_scale(own_key, extent, shards, -0.22, 0.18)
    return jnp.clip(spiked(values, jax.random.fold_in(own_key, 3), *heavy), -reach, reach).astype(kind)


def setup_inputs(seed: int = 0) -> dict:
    key_of = jax.random.split(jax.random.key(seed), 7)
    queries = draw_queries(jax.random.fold_in(key_of[6], 71), 0)
    keys = draw_keys(jax.random.fold_in(key_of[6], 71), 0)
    values = bell_draw(key_of[2], (TOKENS, D), 1.0, 6.0, ((0, 64), (1, 8)))
    dates = draw_dates(jax.random.fold_in(key_of[6], 71), 0)
    plan = draw_plan(jax.random.fold_in(key_of[6], 71), 0)
    out_weight = bell_draw_with(key_of[5], (D, D), D ** -0.5, 0.1875, ((0, 8),), (0, 1, 8, 2.0))
    return {"queries": queries, "keys": keys, "values": values, "dates": dates, "plan": plan, "out_weight": out_weight}


masked_value = -1e30


def take_block(array, block):
    return lax.dynamic_slice_in_dim(array, (block * TOK_DEV).astype(jnp.int32), TOK_DEV, 0)


def block_attention(index, queries, keys, values, dates, plan):
    partners = [index] + [jnp.bitwise_xor(index, plan[turn]).astype(jnp.int32) for turn in range(ROUNDS)]
    query_block = take_block(queries, index).astype(jnp.float32).reshape(TOK_DEV, HEADS, HEAD_DIM)
    query_dates = take_block(dates, index)
    key_rows = jnp.concatenate([take_block(keys, p) for p in partners], 0).astype(jnp.float32)
    value_rows = jnp.concatenate([take_block(values, p) for p in partners], 0).astype(jnp.float32)
    key_dates = jnp.concatenate([take_block(dates, p) for p in partners], 0)
    key_rows = key_rows.reshape(-1, HEADS, HEAD_DIM)
    value_rows = value_rows.reshape(-1, HEADS, HEAD_DIM)
    scores = jnp.einsum("qhd,khd->hqk", query_block, key_rows) * (HEAD_DIM ** -0.5)
    visible = key_dates[None, None, :] <= query_dates[None, :, None]
    scores = jnp.where(visible, scores, masked_value)
    row_max = jnp.max(scores, axis=-1, keepdims=True)
    weights = jnp.where(visible, jnp.exp(scores - row_max), 0.0)
    row_sum = jnp.sum(weights, axis=-1)
    rounded = lax.optimization_barrier(weights.astype(jnp.bfloat16)).astype(jnp.float32)
    attended = jnp.einsum("hqk,khd->qhd", rounded, value_rows) / jnp.transpose(row_sum)[:, :, None]
    return attended.astype(jnp.bfloat16).reshape(TOK_DEV, D)


def reference(queries, keys, values, dates, plan, out_weight):
    blocks = lax.map(lambda index: block_attention(index, queries, keys, values, dates, plan),
                     jnp.arange(N_CTX, dtype=jnp.int32))
    attended = blocks.reshape(TOKENS, D)
    group_width = D // N_HEAD
    summed = jnp.zeros((TOKENS, D), jnp.float32)
    for group in range(N_HEAD):
        partial_term = jnp.dot(attended[:, group * group_width:(group + 1) * group_width],
                               out_weight[group * group_width:(group + 1) * group_width],
                               preferred_element_type=jnp.float32)
        summed = summed + lax.optimization_barrier(partial_term.astype(jnp.bfloat16)).astype(jnp.float32)
    return summed.astype(jnp.bfloat16)
```

```python
import functools

import jax
import jax.numpy as jnp
from jax import lax
from jax.experimental import pallas as pl
from jax.experimental.pallas import tpu as pltpu
from jax.sharding import PartitionSpec as P

MESH = pl.DeviceIdType.MESH
ROWS = 512
HD = 128
NCH = 8
CROWS = ROWS // 2
WINDOW = 2
CHUNK = 128
STEPS = ROWS // CHUNK
X_PEERS = (16, 32, 48)
Z_PEERS = (2, 4, 6)
SHARE = (1, 16, 17, 32, 33, 48, 49)
EXP_SCALE = HD ** -0.5 * 1.4426950408889634
HIDDEN = -float(2 ** 30)
LOWEST = -3e38


def kernel(zstep, plan_ref, q_ref, k_ref, v_ref, d_ref, w_ref, o_ref,
           qx, kx, vx, marks, kv, kvp, farp, st1, xr, st2,
           dk, dkp, dfarp, dst1, dxr, dst2, m_ref, acc,
           om, op, wp, own, ys, yr,
           s63, r63, sc, rc, sp, rp, sx, rx, szh, rzh, sz, rz,
           sw, rw, sl, rl, sg, rg, sy, ry, credit):
    f32, bf = jnp.float32, jnp.bfloat16
    c, h = lax.axis_index("ctx"), lax.axis_index("head")
    y, zhi = h // 2, h % 2
    zlo = (c // 2) % 8
    depth = jnp.where(zlo < 4, zlo, 7 - zlo)
    far, twin, mate = (c ^ 63, h), (c, h ^ 1), (c ^ 1, h)
    over = (c ^ 14, h ^ 1)
    peers = [far, twin] + [(c, (h + 2 * j) % 8) for j in (1, 2, 3)]
    peers += [(c ^ t, h) for t in SHARE + Z_PEERS]

    barrier = pltpu.get_barrier_semaphore()
    for peer in peers:
        pl.semaphore_signal(barrier, inc=1, device_id=peer, device_id_type=MESH)

    @pl.when(depth == 0)
    def _():
        pl.semaphore_signal(barrier, inc=1, device_id=over, device_id_type=MESH)

    dk[0, 0, 0:4, :] = d_ref[...].astype(f32).astype(bf)
    dk[0, 0, 4:16, :] = jnp.zeros((12, 128), bf)
    for n in range(NCH):
        hh, which, sub = n // 4, (n // 2) % 2, n % 2
        src = (k_ref, v_ref)[which]
        kv[0, n] = src[sub * CROWS:(sub + 1) * CROWS, hh * HD:(hh + 1) * HD]
    date_ids = lax.broadcasted_iota(jnp.int32, (HD, ROWS), 0).astype(f32)

    def row_dates(s):
        block = dk[s, 0].astype(f32)
        return jnp.concatenate([block[i:i + 1, :] for i in range(4)], axis=1)

    def key_marks(s):
        marks[s] = jnp.transpose(jnp.where(row_dates(s) > date_ids, HIDDEN, 0.0)).astype(bf)

    query_marks = jnp.transpose(jnp.where(row_dates(0) == date_ids, 1.0, 0.0)).astype(bf)
    for hh in range(2):
        qx[hh, :, 0:HD] = q_ref[:, hh * HD:(hh + 1) * HD]
        qx[hh, :, HD:] = query_marks
    key_marks(0)
    vx[:, HD:] = jnp.ones((ROWS, HD), bf)
    m_ref[...] = jnp.full(m_ref.shape, LOWEST, f32)
    acc[...] = jnp.zeros(acc.shape, f32)

    other = plan_ref[0] ^ plan_ref[1] ^ 63
    crosses = (other >> 3) & 1
    pattern = other ^ (crosses * 63)
    core_bit, x_bits = pattern & 1, (pattern >> 4) & 3

    pl.semaphore_wait(barrier, len(peers) + jnp.where(depth == 0, 1, 0))

    def remote(src, dst, ss, rs, dev):
        return pltpu.make_async_remote_copy(src_ref=src, dst_ref=dst, send_sem=ss, recv_sem=rs,
                                            device_id=dev, device_id_type=MESH)

    data = (kv, kvp, farp, st1, xr, st2)
    date = (dk, dkp, dfarp, dst1, dxr, dst2)

    def to_far(b, n, i):
        return remote(b[0].at[0, n], b[0].at[1, n], s63.at[i], r63.at[i], far)

    def own_to_mate(b, i):
        return remote(b[0].at[0], b[1], sp.at[i], rp.at[i], mate)

    def far_to_mate(b, n, i):
        return remote(b[0].at[1, n], b[2].at[n], sc.at[i], rc.at[i], mate)

    def to_x(b, n, i, j):
        return remote(b[3].at[n], b[4].at[j, n], sx.at[j, i], rx.at[j, i], (c ^ X_PEERS[j], h))

    def to_z(b, n, i):
        return remote(b[5].at[n], b[0].at[2, n], szh.at[i], rzh.at[i], (c ^ zstep, h))

    def pick(flag, one, zero):
        return jnp.where(jnp.full(one.shape, flag, jnp.int32) == 1, one, zero)

    def get(ref, *at):
        return ref[at].astype(f32)

    def stage_x(b, n, i):
        far_to_mate(b, n, i).wait_recv()
        mine = pick(crosses, get(b[0], 1, n), get(b[0], 0, n))
        mates = pick(crosses, get(b[2], n), get(b[1], n))
        b[3][n] = pick(core_bit, mates, mine).astype(bf)
        for j in range(3):
            to_x(b, n, i, j).start()

    def stage_z(b, n, i):
        for j in range(3):
            to_x(b, n, i, j).wait_recv()
        low = pick(x_bits & 1, get(b[4], 0, n), get(b[3], n))
        high = pick(x_bits & 1, get(b[4], 2, n), get(b[4], 1, n))
        picked = pick(x_bits >> 1, high, low).astype(bf)
        if zstep:
            b[5][n] = picked
            to_z(b, n, i).start()
        else:
            b[0][2, n] = picked

    share = pl.ds(pl.multiple_of(((c // 16) * 2 + c % 2) * 32, 32), 32)

    def w_over(j):
        cols = pl.ds(pl.multiple_of((2 * j + 1 - zhi) * 256, 256), 256)
        return remote(w_ref.at[share, cols], wp.at[share, pl.ds(j * 256, 256)], sw.at[j], rw.at[j], over)

    def w_along():
        return remote(wp.at[share], wp.at[share], sl, rl, (c ^ jnp.where(depth == 1, 6, 2), h))

    def w_spread(j):
        return remote(wp.at[share], wp.at[share], sg.at[j], rg.at[j], (c ^ SHARE[j], h))

    def attend(s, hh):
        for sub in range(2):
            rows = slice(sub * CROWS, (sub + 1) * CROWS)
            kx[rows, 0:HD] = kv[s, 4 * hh + sub]
            vx[rows, 0:HD] = kv[s, 4 * hh + 2 + sub]
        kx[:, HD:] = marks[s]

        def step(i, _):
            rows = pl.ds(pl.multiple_of(i * CHUNK, CHUNK), CHUNK)
            scores = lax.dot_general(qx[hh, rows, :], kx[...], (((1,), (1,)), ((), ())),
                                     preferred_element_type=f32)
            old = m_ref[hh, rows, :]
            new = jnp.maximum(old, jnp.max(scores, axis=1, keepdims=True))
            p = jnp.exp2((scores - new[:, 0:1]) * EXP_SCALE).astype(bf)
            decay = jnp.exp2((old - new) * EXP_SCALE)
            acc[hh, rows, :] = (acc[hh, rows, :] * jnp.concatenate([decay, decay], axis=1)
                                + jnp.dot(p, vx[...], preferred_element_type=f32))
            m_ref[hh, rows, :] = new
            return 0

        lax.fori_loop(0, STEPS, step, 0)

    def loop(low, high, body):
        lax.fori_loop(low, high, lambda i, _: (body(i), 0)[1], 0)

    to_far(date, 0, NCH).start()
    for n in range(WINDOW):
        to_far(data, n, n).start()
    own_to_mate(date, 1).start()
    own_to_mate(data, 0).start()

    @pl.when(depth == 0)
    def _():
        for j in range(4):
            w_over(j).start()

    loop(0, 2, lambda hh: attend(0, hh))

    own_to_mate(date, 1).wait_recv()
    own_to_mate(data, 0).wait_recv()
    to_far(date, 0, NCH).wait_recv()
    far_to_mate(date, 0, NCH).start()
    key_marks(1)
    stage_x(date, 0, NCH)

    def pump(n):
        to_far(data, n, n).wait_recv()
        far_to_mate(data, n, n).start()

        @pl.when(n + WINDOW < NCH)
        def _():
            @pl.when(depth == 3)
            def _():
                for t in Z_PEERS:
                    pl.semaphore_signal(credit, inc=1, device_id=(c ^ t, h), device_id_type=MESH)

            @pl.when(depth < 3)
            def _():
                pl.semaphore_wait(credit, 1)

            to_far(data, n + WINDOW, n + WINDOW).start()

        @pl.when(n == depth)
        def _():
            @pl.when(depth == 0)
            def _():
                for j in range(4):
                    w_over(j).wait_recv()

            @pl.when(depth > 0)
            def _():
                w_along().wait_recv()

            @pl.when(depth < 3)
            def _():
                w_along().start()

            for j in range(len(SHARE)):
                w_spread(j).start()

        stage_x(data, n, n)

        @pl.when(n > 0)
        def _():
            stage_z(data, n - 1, n - 1)

    def send_o(hh, i):
        rows = pl.ds(pl.multiple_of(i * CHUNK, CHUNK), CHUNK)
        return remote(om.at[hh, rows], op.at[hh, rows], sz.at[hh, i], rz.at[hh, i], twin)

    def per_head(hh):
        loop(6 * hh, 4 + 4 * hh, pump)

        @pl.when(hh == 0)
        def _():
            stage_z(date, 0, NCH)

        @pl.when(hh == 1)
        def _():
            stage_z(data, NCH - 1, NCH - 1)
            loop(0, STEPS, lambda i: send_o(0, i).start())

        def per_block(s):
            @pl.when(s == 2)
            def _():
                loop(4 + 4 * hh, 6 + 2 * hh, pump)
                if zstep:
                    @pl.when(hh == 0)
                    def _():
                        to_z(date, 0, NCH).wait_recv()

                    loop(4 * hh, 4 * hh + 4, lambda n: to_z(data, n, n).wait_recv())

                @pl.when(hh == 0)
                def _():
                    key_marks(2)

            attend(s, hh)

        loop(1, 3, per_block)

        def close(i):
            rows = pl.ds(pl.multiple_of(i * CHUNK, CHUNK), CHUNK)
            om[hh, rows, :] = (acc[hh, rows, 0:HD] / acc[hh, rows, HD:]).astype(bf)

            @pl.when(hh == 1)
            def _():
                send_o(1, i).start()

        loop(0, STEPS, close)

    loop(0, 2, per_head)

    for j, t in enumerate(SHARE):
        peer = c ^ t
        got = wp.at[pl.ds(pl.multiple_of(((peer // 16) * 2 + peer % 2) * 32, 32), 32)]
        remote(got, got, sg.at[j], rg.at[j], (peer, h)).wait_recv()

    def to_y(j, i):
        return remote(ys.at[j - 1, i], yr.at[j - 1, i], sy.at[j - 1, i], ry.at[j - 1, i],
                      (c, (h + 2 * j) % 8))

    def project(i):
        rows = pl.ds(pl.multiple_of(i * CHUNK, CHUNK), CHUNK)
        send_o(0, i).wait_recv()
        send_o(1, i).wait_recv()

        def group(j):
            g = (y + j) % 4
            cols = pl.ds(pl.multiple_of((2 * g + zhi) * 256, 256), 256)
            pcols = pl.ds(pl.multiple_of(g * 256, 256), 256)
            mine = jnp.concatenate([om[0, rows, :], om[1, rows, :]], axis=1)
            theirs = jnp.concatenate([op[0, rows, :], op[1, rows, :]], axis=1)
            part = (jnp.dot(mine, w_ref[:, cols], preferred_element_type=f32)
                    + jnp.dot(theirs, wp[:, pcols], preferred_element_type=f32))

            @pl.when(j < 4)
            def _():
                ys[j - 1, i] = part.astype(bf)
                to_y(j, i).start()

            @pl.when(j == 4)
            def _():
                own[i] = part

        loop(1, 5, group)

    loop(0, STEPS, project)

    def finish(i):
        rows = pl.ds(pl.multiple_of(i * CHUNK, CHUNK), CHUNK)
        total = own[i]
        for j in (1, 2, 3):
            to_y(j, i).wait_recv()
            total = total + get(yr, j - 1, i)
        o_ref[rows, :] = total.astype(bf)

    loop(0, STEPS, finish)

    def left(b, n, i):
        to_far(b, n, i).wait_send()
        far_to_mate(b, n, i).wait_send()
        for j in range(3):
            to_x(b, n, i, j).wait_send()
        if zstep:
            to_z(b, n, i).wait_send()

    left(date, 0, NCH)
    loop(0, NCH, lambda n: left(data, n, n))
    own_to_mate(date, 1).wait_send()
    own_to_mate(data, 0).wait_send()

    @pl.when(depth == 0)
    def _():
        for j in range(4):
            w_over(j).wait_send()

    @pl.when(depth < 3)
    def _():
        w_along().wait_send()

    for j in range(len(SHARE)):
        w_spread(j).wait_send()

    def rest(i):
        for hh in range(2):
            send_o(hh, i).wait_send()
        for j in (1, 2, 3):
            to_y(j, i).wait_send()

    loop(0, STEPS, rest)


def call(zstep, number):
    bf, f32 = jnp.bfloat16, jnp.float32
    dma = pltpu.SemaphoreType.DMA
    vmem = pl.BlockSpec(memory_space=pltpu.VMEM)
    smem = pl.BlockSpec(memory_space=pltpu.SMEM)
    piece, dates = (CROWS, HD), (16, HD)
    return pl.pallas_call(
        functools.partial(kernel, zstep),
        out_shape=jax.ShapeDtypeStruct((ROWS, 256), bf),
        in_specs=[smem, vmem, vmem, vmem, vmem, vmem],
        out_specs=vmem,
        scratch_shapes=[
            pltpu.VMEM((2, ROWS, 256), bf),
            pltpu.VMEM((ROWS, 256), bf),
            pltpu.VMEM((ROWS, 256), bf),
            pltpu.VMEM((3, ROWS, HD), bf),
            pltpu.VMEM((3, NCH) + piece, bf),
            pltpu.VMEM((NCH,) + piece, bf),
            pltpu.VMEM((NCH,) + piece, bf),
            pltpu.VMEM((NCH,) + piece, bf),
            pltpu.VMEM((3, NCH) + piece, bf),
            pltpu.VMEM((NCH,) + piece, bf),
            pltpu.VMEM((3, 1) + dates, bf),
            pltpu.VMEM((1,) + dates, bf),
            pltpu.VMEM((1,) + dates, bf),
            pltpu.VMEM((1,) + dates, bf),
            pltpu.VMEM((3, 1) + dates, bf),
            pltpu.VMEM((1,) + dates, bf),
            pltpu.VMEM((2, ROWS, HD), f32),
            pltpu.VMEM((2, ROWS, 256), f32),
            pltpu.VMEM((2, ROWS, HD), bf),
            pltpu.VMEM((2, ROWS, HD), bf),
            pltpu.VMEM((256, 1024), bf),
            pltpu.VMEM((STEPS, CHUNK, 256), f32),
            pltpu.VMEM((3, STEPS, CHUNK, 256), bf),
            pltpu.VMEM((3, STEPS, CHUNK, 256), bf),
            dma((NCH + 1,)), dma((NCH + 1,)), dma((NCH + 1,)), dma((NCH + 1,)), dma((2,)), dma((2,)),
            dma((3, NCH + 1)), dma((3, NCH + 1)), dma((NCH + 1,)), dma((NCH + 1,)),
            dma((2, STEPS)), dma((2, STEPS)), dma((4,)), dma((4,)), dma, dma,
            dma((len(SHARE),)), dma((len(SHARE),)), dma((3, STEPS)), dma((3, STEPS)),
            pltpu.SemaphoreType.REGULAR,
        ],
        compiler_params=pltpu.CompilerParams(
            collective_id=number, has_side_effects=True, vmem_limit_bytes=48 << 20),
        cost_estimate=pl.CostEstimate(flops=1_400_000_000, bytes_accessed=3 << 20,
                                      transcendentals=1_600_000),
    )


def on_device(queries, keys, values, dates, plan, out_weight):
    other = plan[0] ^ plan[1] ^ 63
    bits = (other >> 1) & 7
    z_index = jnp.where(bits >= 4, 7 - bits, bits)
    calls = [call(2 * i, i) for i in range(4)]
    return lax.switch(z_index, calls, plan, queries, keys, values, dates.reshape(4, 128), out_weight)


def solution(mesh):
    return jax.shard_map(
        on_device,
        mesh=mesh,
        in_specs=(P("ctx", "head"), P("ctx", "head"), P("ctx", "head"), P("ctx"), P(), P("head", None)),
        out_specs=P("ctx", "head"),
        check_vma=False,
    )
```

```python
import functools

import jax
import jax.numpy as jnp
from jax import lax
from jax.experimental import pallas as pl
from jax.experimental.pallas import tpu as pltpu
from jax.sharding import PartitionSpec as P

MESH = pl.DeviceIdType.MESH
ROWS = 512
HD = 128
NCH = 8
CROWS = ROWS // 2
WINDOW = 3
CHUNK = 128
STEPS = ROWS // CHUNK
BLOCK = 256
Z_PEERS = (2, 4, 6)
SHARE = (1, 16, 17, 32, 33, 48, 49)
EXP_SCALE = HD ** -0.5 * 1.4426950408889634
HIDDEN = -float(2 ** 30)
LOWEST = -3e38


def kernel(step, plan_ref, q_ref, k_ref, v_ref, d_ref, w_ref, o_ref,
           qx, kx, vx, marks, kv, kvp, farp, st,
           dk, dkp, dfarp, dst, m_ref, acc,
           om, op, wp, own, ys, yr,
           s63, r63, sc, rc, sp, rp, so, ro, sz, rz,
           sw, rw, sl, rl, sg, rg, sy, ry, credit):
    f32, bf = jnp.float32, jnp.bfloat16
    c, h = lax.axis_index("ctx"), lax.axis_index("head")
    y, zhi = h // 2, h % 2
    zlo = (c // 2) % 8
    depth = jnp.where(zlo < 4, zlo, 7 - zlo)
    far, twin, mate = (c ^ 63, h), (c, h ^ 1), (c ^ 1, h)
    over = (c ^ 14, h ^ 1)
    peers = [far, twin] + [(c, (h + 2 * j) % 8) for j in (1, 2, 3)]
    peers += [(c ^ t, h) for t in sorted({step, *SHARE, *Z_PEERS} - {0})]

    barrier = pltpu.get_barrier_semaphore()
    for peer in peers:
        pl.semaphore_signal(barrier, inc=1, device_id=peer, device_id_type=MESH)

    @pl.when(depth == 0)
    def _():
        pl.semaphore_signal(barrier, inc=1, device_id=over, device_id_type=MESH)

    dk[0, 0, 0:4, :] = d_ref[...].astype(f32).astype(bf)
    dk[0, 0, 4:16, :] = jnp.zeros((12, 128), bf)
    for n in range(NCH):
        hh, which, sub = n // 4, (n // 2) % 2, n % 2
        src = (k_ref, v_ref)[which]
        kv[0, n] = src[sub * CROWS:(sub + 1) * CROWS, hh * HD:(hh + 1) * HD]
    date_ids = lax.broadcasted_iota(jnp.int32, (HD, ROWS), 0).astype(f32)

    def row_dates(s):
        block = dk[s, 0].astype(f32)
        return jnp.concatenate([block[i:i + 1, :] for i in range(4)], axis=1)

    def key_marks(s):
        marks[s] = jnp.transpose(jnp.where(row_dates(s) > date_ids, HIDDEN, 0.0)).astype(bf)

    query_marks = jnp.transpose(jnp.where(row_dates(0) == date_ids, 1.0, 0.0)).astype(bf)
    for hh in range(2):
        qx[hh, :, 0:HD] = q_ref[:, hh * HD:(hh + 1) * HD]
        qx[hh, :, HD:] = query_marks
    key_marks(0)
    vx[:, HD:] = jnp.ones((ROWS, HD), bf)
    m_ref[...] = jnp.full(m_ref.shape, LOWEST, f32)
    acc[...] = jnp.zeros(acc.shape, f32)

    other = plan_ref[0] ^ plan_ref[1] ^ 63
    crosses = (other >> 3) & 1
    pattern = other ^ (crosses * 63)
    core_bit = pattern & 1

    pl.semaphore_wait(barrier, len(peers) + jnp.where(depth == 0, 1, 0))

    def remote(src, dst, ss, rs, dev):
        return pltpu.make_async_remote_copy(src_ref=src, dst_ref=dst, send_sem=ss, recv_sem=rs,
                                            device_id=dev, device_id_type=MESH)

    data = (kv, kvp, farp, st)
    date = (dk, dkp, dfarp, dst)

    def to_far(b, n, i):
        return remote(b[0].at[0, n], b[0].at[1, n], s63.at[i], r63.at[i], far)

    def own_to_mate(b, i):
        return remote(b[0].at[0], b[1], sp.at[i], rp.at[i], mate)

    def far_to_mate(b, n, i):
        return remote(b[0].at[1, n], b[2].at[n], sc.at[i], rc.at[i], mate)

    def to_other(b, n, i):
        return remote(b[3].at[n], b[0].at[2, n], so.at[i], ro.at[i], (c ^ step, h))

    def pick(flag, one, zero):
        return jnp.where(jnp.full(one.shape, flag, jnp.int32) == 1, one, zero)

    def get(ref, *at):
        return ref[at].astype(f32)

    def stage(b, n, i):
        far_to_mate(b, n, i).wait_recv()
        mine = pick(crosses, get(b[0], 1, n), get(b[0], 0, n))
        mates = pick(crosses, get(b[2], n), get(b[1], n))
        picked = pick(core_bit, mates, mine).astype(bf)
        if step:
            b[3][n] = picked
            to_other(b, n, i).start()
        else:
            b[0][2, n] = picked

    share = pl.ds(pl.multiple_of(((c // 16) * 2 + c % 2) * 32, 32), 32)

    def w_over(j):
        cols = pl.ds(pl.multiple_of((2 * j + 1 - zhi) * 256, 256), 256)
        return remote(w_ref.at[share, cols], wp.at[share, pl.ds(j * 256, 256)], sw.at[j], rw.at[j], over)

    def w_along():
        return remote(wp.at[share], wp.at[share], sl, rl, (c ^ jnp.where(depth == 1, 6, 2), h))

    def w_spread(j):
        return remote(wp.at[share], wp.at[share], sg.at[j], rg.at[j], (c ^ SHARE[j], h))

    def attend(s, hh):
        for sub in range(2):
            rows = slice(sub * CROWS, (sub + 1) * CROWS)
            kx[rows, 0:HD] = kv[s, 4 * hh + sub]
            vx[rows, 0:HD] = kv[s, 4 * hh + 2 + sub]
        kx[:, HD:] = marks[s]

        def queries(i, _):
            rows = pl.ds(pl.multiple_of(i * BLOCK, BLOCK), BLOCK)
            scores = lax.dot_general(qx[hh, rows, :], kx[...], (((1,), (1,)), ((), ())),
                                     preferred_element_type=f32)
            old = m_ref[hh, rows, :]
            new = jnp.maximum(old, jnp.max(scores, axis=1, keepdims=True))
            p = jnp.exp2((scores - new[:, 0:1]) * EXP_SCALE).astype(bf)
            decay = jnp.exp2((old - new) * EXP_SCALE)
            acc[hh, rows, :] = (acc[hh, rows, :] * jnp.concatenate([decay, decay], axis=1)
                                + jnp.dot(p, vx[...], preferred_element_type=f32))
            m_ref[hh, rows, :] = new
            return 0

        lax.fori_loop(0, ROWS // BLOCK, queries, 0)

    def loop(low, high, body):
        lax.fori_loop(low, high, lambda i, _: (body(i), 0)[1], 0)

    to_far(date, 0, NCH).start()
    for n in range(WINDOW):
        to_far(data, n, n).start()
    own_to_mate(date, 1).start()
    own_to_mate(data, 0).start()

    @pl.when(depth == 0)
    def _():
        for j in range(4):
            w_over(j).start()

    def first_dates():
        own_to_mate(date, 1).wait_recv()
        own_to_mate(data, 0).wait_recv()
        to_far(date, 0, NCH).wait_recv()
        far_to_mate(date, 0, NCH).start()
        key_marks(1)
        stage(date, 0, NCH)

    def pump(n):
        to_far(data, n, n).wait_recv()
        far_to_mate(data, n, n).start()

        @pl.when(n + WINDOW < NCH)
        def _():
            @pl.when(depth == 3)
            def _():
                for t in Z_PEERS:
                    pl.semaphore_signal(credit, inc=1, device_id=(c ^ t, h), device_id_type=MESH)

            @pl.when(depth < 3)
            def _():
                pl.semaphore_wait(credit, 1)

            to_far(data, n + WINDOW, n + WINDOW).start()

        @pl.when(n == depth)
        def _():
            @pl.when(depth == 0)
            def _():
                for j in range(4):
                    w_over(j).wait_recv()

            @pl.when(depth > 0)
            def _():
                w_along().wait_recv()

            @pl.when(depth < 3)
            def _():
                w_along().start()

            for j in range(len(SHARE)):
                w_spread(j).start()

        stage(data, n, n)

    def send_o(hh, i):
        rows = pl.ds(pl.multiple_of(i * CHUNK, CHUNK), CHUNK)
        return remote(om.at[hh, rows], op.at[hh, rows], sz.at[hh, i], rz.at[hh, i], twin)

    def per_head(hh):
        def per_block(s):
            @pl.when((hh == 0) & (s == 1))
            def _():
                first_dates()

            @pl.when(s > 0)
            def _():
                loop(6 * hh + (s - 1) * (4 - 2 * hh), 4 + 4 * hh + (s - 1) * (2 - 2 * hh), pump)

            @pl.when((hh == 1) & (s == 1))
            def _():
                loop(0, STEPS, lambda i: send_o(0, i).start())

            @pl.when(s == 2)
            def _():
                if step:
                    @pl.when(hh == 0)
                    def _():
                        to_other(date, 0, NCH).wait_recv()

                    loop(4 * hh, 4 * hh + 4, lambda n: to_other(data, n, n).wait_recv())

                @pl.when(hh == 0)
                def _():
                    key_marks(2)

            attend(s, hh)

        loop(0, 3, per_block)

        def close(i):
            rows = pl.ds(pl.multiple_of(i * CHUNK, CHUNK), CHUNK)
            om[hh, rows, :] = (acc[hh, rows, 0:HD] / acc[hh, rows, HD:]).astype(bf)

            @pl.when(hh == 1)
            def _():
                send_o(1, i).start()

        loop(0, STEPS, close)

    loop(0, 2, per_head)

    for j, t in enumerate(SHARE):
        peer = c ^ t
        got = wp.at[pl.ds(pl.multiple_of(((peer // 16) * 2 + peer % 2) * 32, 32), 32)]
        remote(got, got, sg.at[j], rg.at[j], (peer, h)).wait_recv()

    def to_y(j, i):
        return remote(ys.at[j - 1, i], yr.at[j - 1, i], sy.at[j - 1, i], ry.at[j - 1, i],
                      (c, (h + 2 * j) % 8))

    def project(i):
        rows = pl.ds(pl.multiple_of(i * CHUNK, CHUNK), CHUNK)
        send_o(0, i).wait_recv()
        send_o(1, i).wait_recv()

        def group(j):
            g = (y + j) % 4
            cols = pl.ds(pl.multiple_of((2 * g + zhi) * 256, 256), 256)
            pcols = pl.ds(pl.multiple_of(g * 256, 256), 256)
            mine = jnp.concatenate([om[0, rows, :], om[1, rows, :]], axis=1)
            theirs = jnp.concatenate([op[0, rows, :], op[1, rows, :]], axis=1)
            part = (jnp.dot(mine, w_ref[:, cols], preferred_element_type=f32)
                    + jnp.dot(theirs, wp[:, pcols], preferred_element_type=f32))

            @pl.when(j < 4)
            def _():
                ys[j - 1, i] = part.astype(bf)
                to_y(j, i).start()

            @pl.when(j == 4)
            def _():
                own[i] = part

        loop(1, 5, group)

    loop(0, STEPS, project)

    def finish(i):
        rows = pl.ds(pl.multiple_of(i * CHUNK, CHUNK), CHUNK)
        total = own[i]
        for j in (1, 2, 3):
            to_y(j, i).wait_recv()
            total = total + get(yr, j - 1, i)
        o_ref[rows, :] = total.astype(bf)

    loop(0, STEPS, finish)

    def left(b, n, i):
        to_far(b, n, i).wait_send()
        far_to_mate(b, n, i).wait_send()
        if step:
            to_other(b, n, i).wait_send()

    left(date, 0, NCH)
    loop(0, NCH, lambda n: left(data, n, n))
    own_to_mate(date, 1).wait_send()
    own_to_mate(data, 0).wait_send()

    @pl.when(depth == 0)
    def _():
        for j in range(4):
            w_over(j).wait_send()

    @pl.when(depth < 3)
    def _():
        w_along().wait_send()

    for j in range(len(SHARE)):
        w_spread(j).wait_send()

    def rest(i):
        for hh in range(2):
            send_o(hh, i).wait_send()
        for j in (1, 2, 3):
            to_y(j, i).wait_send()

    loop(0, STEPS, rest)


def call(step, number):
    bf, f32 = jnp.bfloat16, jnp.float32
    dma = pltpu.SemaphoreType.DMA
    vmem = pl.BlockSpec(memory_space=pltpu.VMEM)
    smem = pl.BlockSpec(memory_space=pltpu.SMEM)
    piece, dates = (CROWS, HD), (16, HD)
    return pl.pallas_call(
        functools.partial(kernel, step),
        out_shape=jax.ShapeDtypeStruct((ROWS, 256), bf),
        in_specs=[smem, vmem, vmem, vmem, vmem, vmem],
        out_specs=vmem,
        scratch_shapes=[
            pltpu.VMEM((2, ROWS, 256), bf),
            pltpu.VMEM((ROWS, 256), bf),
            pltpu.VMEM((ROWS, 256), bf),
            pltpu.VMEM((3, ROWS, HD), bf),
            pltpu.VMEM((3, NCH) + piece, bf),
            pltpu.VMEM((NCH,) + piece, bf),
            pltpu.VMEM((NCH,) + piece, bf),
            pltpu.VMEM((NCH,) + piece, bf),
            pltpu.VMEM((3, 1) + dates, bf),
            pltpu.VMEM((1,) + dates, bf),
            pltpu.VMEM((1,) + dates, bf),
            pltpu.VMEM((1,) + dates, bf),
            pltpu.VMEM((2, ROWS, HD), f32),
            pltpu.VMEM((2, ROWS, 256), f32),
            pltpu.VMEM((2, ROWS, HD), bf),
            pltpu.VMEM((2, ROWS, HD), bf),
            pltpu.VMEM((256, 1024), bf),
            pltpu.VMEM((STEPS, CHUNK, 256), f32),
            pltpu.VMEM((3, STEPS, CHUNK, 256), bf),
            pltpu.VMEM((3, STEPS, CHUNK, 256), bf),
            dma((NCH + 1,)), dma((NCH + 1,)), dma((NCH + 1,)), dma((NCH + 1,)), dma((2,)), dma((2,)),
            dma((NCH + 1,)), dma((NCH + 1,)), dma((2, STEPS)), dma((2, STEPS)), dma((4,)), dma((4,)), dma, dma,
            dma((len(SHARE),)), dma((len(SHARE),)), dma((3, STEPS)), dma((3, STEPS)),
            pltpu.SemaphoreType.REGULAR,
        ],
        compiler_params=pltpu.CompilerParams(
            collective_id=number, has_side_effects=True, vmem_limit_bytes=48 << 20),
        cost_estimate=pl.CostEstimate(flops=1_400_000_000, bytes_accessed=3 << 20,
                                      transcendentals=1_600_000),
    )


def on_device(queries, keys, values, dates, plan, out_weight):
    other = plan[0] ^ plan[1] ^ 63
    pattern = jnp.where((other >> 3) & 1 == 1, other ^ 63, other)
    index = ((pattern >> 4) << 2) | ((pattern >> 1) & 3)
    calls = [call((i // 4) * 16 + (i % 4) * 2, i) for i in range(16)]
    return lax.switch(index, calls, plan, queries, keys, values, dates.reshape(4, 128), out_weight)


def solution(mesh):
    return jax.shard_map(
        on_device,
        mesh=mesh,
        in_specs=(P("ctx", "head"), P("ctx", "head"), P("ctx", "head"), P("ctx"), P(), P("head", None)),
        out_specs=P("ctx", "head"),
        check_vma=False,
    )
```
